32 devices in a mesh: groups: 2 (over x), row: 16 (over z, y, core).
Axes of the slice: x: 2, y: 2, z: 4, core: 2. Of those that a mesh axis runs over, the one named last changes fastest.
Arguments:
- active_ids: int32 [256], P(('groups', 'row')), parts along dimension 0, may hold values from 0 to 2047, as said below
- active_layers: int32 [256], P(('groups', 'row')), parts along dimension 0, may hold values from 0 to 15, as said below
- activations: float32 [256], P(('groups', 'row')), parts along dimension 0, may hold values from 0.1 to 10
- kept_tiles: int32 [32, 4], P('groups'), parts along dimension 0, may hold values 0 or 1
- owner_map: int32 [4096], P('groups'), parts along dimension 0, may hold values from 0 to 2047, as said below
- dict_decoder: bfloat16 [4096, 8192], P(('groups', 'row')), parts along dimension 0, may hold values from -0.0625 to 0.0625
- dict_encoder: bfloat16 [4096, 8192], P(('groups', 'row')), parts along dimension 0, may hold values from -6 to 6
Outputs:
- edges: float32 [512, 128], P(('groups', 'row')), parts along dimension 0
- weights: float32 [512, 128], P(('groups', 'row')), parts along dimension 0
The draws below stay inside these ranges and needn't reach their ends.
There are 2 independent parts, one for each index of `groups`. The reference program is written for one: setup_inputs(seed, part) draws one part's arguments, and reference() takes and returns one part's arrays. A program takes and returns all parts, laid end to end along the dimension named above; each array names one. Nothing has to cross between parts.
Inputs may be any that keep to these rules, and one draw needn't show every extreme that they name: `active_ids`: distinct ids; within one device's 8 list entries no two ids share an owner (owner_map value // 128); some owner holds exactly 16 of the 128 ids and none more. `active_layers`: non-decreasing along the list. `owner_map`: a permutation: slot s is stored on row device s // 128.
All inputs are finite; a program needn't handle non-finite values.
Results may differ from the reference program's by a relative error of at most 0.0003.
Values may be sent and summed in bfloat16 or wider, within the bound.
A program may use at most 64 MiB of HBM per device.

```python
import math
import jax
import jax.numpy as jnp

D = 8192
F_DEV = 8
DICT_DEV = 128
LAYERS = 16
COL_TILES = 4
FEATS = 128
DICT = 2048
OWN_CAP = 16
N_ROW = 16


def shared_slots(key):
    return jax.random.permutation(key, DICT)


def draw_owner_map(key, part):
    return shared_slots(key).astype(jnp.int32)


def draw_active_ids(key, part):
    slots = shared_slots(key)
    key = jax.random.fold_in(key, 11)
    key_owner, key_offset, key_shuffle, key_rotate = jax.random.split(key, 4)
    position = jnp.arange(FEATS, dtype=jnp.int32)
    first_end = FEATS // 2
    second_end = 3 * FEATS // 4
    rank = jnp.where(position < first_end, position // (2 * F_DEV), jnp.where(position < second_end, N_ROW // 4 + (position - first_end) // F_DEV, N_ROW // 2 + (position - second_end) // (F_DEV // 2)))
    within = jnp.where(position < first_end, position % (2 * F_DEV), jnp.where(position < second_end, (position - first_end) % F_DEV, (position - second_end) % (F_DEV // 2)))
    owner_order = jax.random.permutation(key_owner, N_ROW).astype(jnp.int32)
    owner = owner_order[rank]
    offsets = jax.random.randint(key_offset, (N_ROW,), 0, DICT_DEV, dtype=jnp.int32)
    local_row = (within + offsets[owner]) % DICT_DEV
    inverse = jnp.argsort(slots, stable=True).astype(jnp.int32)
    chosen_ids = inverse[owner * DICT_DEV + local_row]
    rotation = jax.random.randint(key_rotate, (), 0, FEATS, dtype=jnp.int32)
    moved = (position + rotation) % FEATS
    block_number = moved % N_ROW
    inner = moved // N_ROW
    shuffles = jax.vmap(lambda single: jax.random.permutation(single, F_DEV))(jax.random.split(key_shuffle, N_ROW)).astype(jnp.int32)
    target = block_number * F_DEV + shuffles[block_number, inner]
    return jnp.zeros((FEATS,), jnp.int32).at[target].set(chosen_ids)


def draw_active_layers(key, part):
    key = jax.random.fold_in(key, 23)
    return jnp.sort(jax.random.randint(key, (FEATS,), 0, LAYERS, dtype=jnp.int32)).astype(jnp.int32)


def set_ends(drawn, stream_key, smallest, top_value):
    dims = drawn.shape
    spot = [jax.random.randint(jax.random.fold_in(stream_key, axis), (), 0, dims[axis]) for axis in range(len(dims))]
    drawn = drawn.at[tuple(spot)].set(smallest)
    longest = dims.index(max(dims))
    spot[longest] = (spot[longest] + 1) % dims[longest]
    return drawn.at[tuple(spot)].set(top_value)


def shard_levels(own_key, extent, pieces, smallest, high):
    def one(dim, parts):
        draws = jax.random.uniform(jax.random.fold_in(jax.random.fold_in(own_key, 6), dim), (parts,), jnp.float32, smallest / len(pieces), high / len(pieces))
        return jnp.repeat(jnp.exp(draws), extent[dim] // parts).reshape((-1,) + (1,) * (len(extent) - dim - 1))

    factor_of = one(*pieces[0])
    for cut in pieces[1:]:
        factor_of = factor_of * one(*cut)
    return factor_of


def centred(own_key, shape, width, most, cuts=(), kind=jnp.bfloat16):
    array = jax.random.normal(own_key, shape, jnp.float32) * width
    if len(cuts) > 0:
        array = shard_levels(own_key, shape, cuts, -0.22, 0.18) * array
    return jnp.clip(array, min=-most, max=most).astype(kind)


def setup_inputs(seed: int = 0, part: int = 0) -> dict:
    key_of = jax.random.split(jax.random.key(seed), 8)
    part_splits = jax.random.split(jax.random.fold_in(key_of[7], part), 8)
    active_ids = draw_active_ids(jax.random.fold_in(jax.random.fold_in(key_of[7], part), 71), part)
    active_layers = draw_active_layers(jax.random.fold_in(jax.random.fold_in(key_of[7], part), 71), part)
    activations = jnp.clip(jnp.exp(math.log(10.0) - 4.6051702 * jax.random.uniform(part_splits[2], (FEATS,), jnp.float32) ** shard_levels(part_splits[2], (FEATS,), ((0, 16),), -0.2, 0.2)), 0.1, 10.0)
    kept_tiles = set_ends((jax.random.randint(part_splits[3], (N_ROW, COL_TILES), 0, 4) < 3).astype(jnp.int32), jax.random.fold_in(part_splits[3], 1), 0, 1)
    owner_map = draw_owner_map(jax.random.fold_in(jax.random.fold_in(key_of[7], part), 71), part)
    dict_decoder = centred(part_splits[5], (DICT, D), D ** -0.5, 0.0625, ((0, 16),))
    dict_encoder = centred(part_splits[6], (DICT, D), 1.0, 6.0, ((0, 16),))
    return dict(active_ids=active_ids, active_layers=active_layers, activations=activations, kept_tiles=kept_tiles, owner_map=owner_map, dict_decoder=dict_decoder, dict_encoder=dict_encoder)


def reference(active_ids, active_layers, activations, kept_tiles, owner_map, dict_decoder, dict_encoder):
    storage = owner_map[active_ids]
    sources = dict_decoder[storage]
    targets = dict_encoder[storage]
    dots = jnp.dot(sources, targets.T, preferred_element_type=jnp.float32)
    positions = jnp.arange(FEATS, dtype=jnp.int32)
    kept = kept_tiles[positions // F_DEV][:, positions // (FEATS // COL_TILES)]
    allowed = (active_layers[:, None] < active_layers[None, :]) & (kept > 0)
    edge_list = jnp.where(allowed, activations[:, None] * dots, jnp.float32(0))
    magnitude = jnp.abs(edge_list)
    column_total = jnp.sum(magnitude, axis=0)
    column_count = jnp.sum(allowed.astype(jnp.float32), axis=0)
    weight_list = magnitude * jnp.maximum(column_count, 1.0) / jnp.maximum(column_total, 1.0)
    owners = storage // DICT_DEV
    onehot = (owners[:, None] == jnp.arange(N_ROW, dtype=jnp.int32)[None, :]).astype(jnp.int32)
    places = jnp.sum((jnp.cumsum(onehot, axis=0) - onehot) * onehot, axis=1)
    packed_rows = (owners * OWN_CAP + places).astype(jnp.int32)
    edges = jnp.zeros((N_ROW * OWN_CAP, FEATS), jnp.float32).at[packed_rows].set(edge_list)
    weights = jnp.zeros((N_ROW * OWN_CAP, FEATS), jnp.float32).at[packed_rows].set(weight_list)
    return edges, weights
```

```python
import functools

import jax
import jax.numpy as jnp
from jax import lax
from jax.experimental import pallas as pl
from jax.experimental.pallas import tpu as pltpu
from jax.sharding import PartitionSpec as P

MESH = pl.DeviceIdType.MESH


def far_first(n):
    return sorted(range(1, n), key=lambda m: abs(2 * m - n))


def iota(shape, axis):
    return lax.broadcasted_iota(jnp.int32, shape, axis)


def kernel(
    n,
    ids_ref,
    layers_ref,
    acts_ref,
    map_ref,
    kept_ref,
    dec_ref,
    enc_ref,
    edges_ref,
    weights_ref,
    stored_vm,
    meta_out,
    meta_in,
    rows_out,
    rows_in,
    part_out,
    part_in,
    total_out,
    total_in,
    load_sem,
    send_sem,
    recv_sem,
):
    me = lax.axis_index("row")
    mine = ids_ref.shape[0]
    stored, width = dec_ref.shape
    feats = n * mine
    cap = 2 * mine
    chunk = width // n
    offsets = far_first(n)

    loads = [
        pltpu.make_async_copy(dec_ref, stored_vm.at[pl.ds(0, stored)], load_sem.at[0]),
        pltpu.make_async_copy(enc_ref, stored_vm.at[pl.ds(stored, stored)], load_sem.at[1]),
    ]
    for load in loads:
        load.start()

    barrier = pltpu.get_barrier_semaphore()
    for m in offsets:
        pl.semaphore_signal(
            barrier, inc=1, device_id={"row": lax.rem(me + m, n)}, device_id_type=MESH
        )

    lane = iota((8, feats), 1)
    field = iota((8, feats), 0)
    block = jnp.zeros((8, feats), jnp.float32)
    for k in range(mine):
        slot = map_ref[ids_ref[k]]
        here = lane == me * mine + k
        whole = jnp.where(
            field == 0, slot // stored, jnp.where(field == 1, slot % stored, layers_ref[k])
        ).astype(jnp.float32)
        block = jnp.where(here, jnp.where(field == 3, acts_ref[k], whole), block)
    meta_out[...] = block
    meta_in[me] = block

    pl.semaphore_wait(barrier, n - 1)

    def exchange(phase, source, target):
        copies = []
        for m in offsets:
            copy = pltpu.make_async_remote_copy(
                src_ref=source(lax.rem(me + m, n)),
                dst_ref=target,
                send_sem=send_sem.at[phase, m],
                recv_sem=recv_sem.at[phase, m],
                device_id={"row": lax.rem(me + m, n)},
                device_id_type=MESH,
            )
            copy.start()
            copies.append(copy)
        return copies

    first = exchange(0, lambda p: meta_out, meta_in.at[me])
    before = (iota((feats, feats), 0) < iota((feats, feats), 1)).astype(jnp.bfloat16)
    for copy in first:
        copy.wait_recv()
    meta = jnp.sum(meta_in[...], axis=0)
    owner = meta[0:1].astype(jnp.int32)
    local = meta[1:2].astype(jnp.int32)
    layer = meta[2:3]
    act = meta[3:4]
    by_owner = (jnp.broadcast_to(owner, (n, feats)) == iota((n, feats), 0)).astype(jnp.float32)
    earlier = jnp.dot(by_owner.astype(jnp.bfloat16), before, preferred_element_type=jnp.float32)
    place = jnp.sum(by_owner * earlier, axis=0, keepdims=True).astype(jnp.int32)
    packed = jnp.where(owner == me, place, -1)
    chosen = jnp.broadcast_to(packed, (cap, feats)) == iota((cap, feats), 0)
    pick = jnp.sum(
        jnp.where(chosen, jnp.broadcast_to(local + 1, (cap, feats)).astype(jnp.float32), 0.0),
        axis=1,
        keepdims=True,
    )
    pick = jnp.concatenate([pick, pick], axis=0)
    column = iota((2 * cap, 2 * stored), 1)
    second = iota((2 * cap, 2 * stored), 0) >= cap
    sought = jnp.where(second, column - stored, column) + 1
    sought = jnp.where(sought <= 0, -1, jnp.where(sought > stored, -1, sought))
    select = (
        jnp.broadcast_to(pick, (2 * cap, 2 * stored)) == sought.astype(jnp.float32)
    ).astype(jnp.bfloat16)

    for load in loads:
        load.wait()

    def selected(p):
        return jnp.dot(
            select,
            stored_vm[:, pl.ds(pl.multiple_of(p * chunk, chunk), chunk)],
            preferred_element_type=jnp.float32,
        ).astype(jnp.bfloat16)

    def take_and_give(p):
        rows_out[p] = selected(p)
        return rows_out.at[p]

    bulk = exchange(1, take_and_give, rows_in.at[me])
    rows_in[me] = selected(me)

    kept = kept_ref[...]
    tiles, column_tiles = kept.shape
    spread = jnp.zeros((tiles, feats), jnp.int32)
    for c in range(column_tiles):
        within = iota((tiles, feats), 1) // (feats // column_tiles) == c
        spread = jnp.where(within, jnp.broadcast_to(kept[:, c : c + 1], (tiles, feats)), spread)
    spread = jnp.broadcast_to(spread[:, None, :], (tiles, mine, feats)).reshape(feats, feats)
    layer_down = jnp.transpose(jnp.broadcast_to(layer, (feats, feats)))
    allowed = jnp.where(
        layer_down < jnp.broadcast_to(layer, (feats, feats)),
        jnp.where(spread > 0, 1.0, 0.0),
        0.0,
    )
    count = jnp.sum(allowed, axis=0, keepdims=True)
    chosen_f = jnp.where(chosen, 1.0, 0.0)
    allowed_mine = jnp.dot(
        chosen_f.astype(jnp.bfloat16),
        allowed.astype(jnp.bfloat16),
        preferred_element_type=jnp.float32,
    )
    act_mine = jnp.sum(chosen_f * act, axis=1, keepdims=True)
    place_of = owner * cap + place
    position = (
        jnp.broadcast_to(place_of, (n * cap, feats)) == iota((n * cap, feats), 0)
    ).astype(jnp.float32)
    ordering = jnp.transpose(position).astype(jnp.bfloat16)

    for copy in bulk:
        copy.wait_recv()
    sources = rows_in[:, :cap, :].reshape(n * cap, chunk)
    targets = rows_in[:, cap:, :].reshape(n * cap, chunk)
    targets = jnp.dot(ordering, targets, preferred_element_type=jnp.float32).astype(jnp.bfloat16)
    part = lax.dot_general(
        sources, targets, (((1,), (1,)), ((), ())), preferred_element_type=jnp.float32
    )
    part_out[...] = part.reshape(n, cap, feats)
    sums = exchange(2, lambda p: part_out.at[p], part_in.at[me])
    part_in[me] = part_out[me]
    for copy in sums:
        copy.wait_recv()
    dots = jnp.sum(part_in[...], axis=0)
    edges = jnp.where(allowed_mine > 0.0, act_mine * dots, 0.0)
    edges_ref[...] = edges
    magnitude = jnp.abs(edges)
    partial = jnp.sum(magnitude.reshape(cap // 8, 8, feats), axis=0)
    total_out[...] = partial
    total_in[me] = partial
    totals = exchange(3, lambda p: total_out, total_in.at[me])
    for copy in totals:
        copy.wait_recv()
    total = jnp.sum(jnp.sum(total_in[...], axis=0), axis=0, keepdims=True)
    weights_ref[...] = magnitude * jnp.maximum(count, 1.0) / jnp.maximum(total, 1.0)
    for copy in first + bulk + sums + totals:
        copy.wait_send()


def solution(mesh):
    n = mesh.shape["row"]

    def shards(ids, layers, acts, kept, owner_map, decoder, encoder):
        mine = ids.shape[0]
        stored, width = decoder.shape
        feats, cap = n * mine, 2 * mine
        smem = pl.BlockSpec(memory_space=pltpu.SMEM)
        vmem = pl.BlockSpec(memory_space=pltpu.VMEM)
        hbm = pl.BlockSpec(memory_space=pl.ANY)
        result = jax.ShapeDtypeStruct((cap, feats), jnp.float32)
        return pl.pallas_call(
            functools.partial(kernel, n),
            out_shape=(result, result),
            in_specs=[smem, smem, smem, smem, vmem, hbm, hbm],
            out_specs=(vmem, vmem),
            scratch_shapes=[
                pltpu.VMEM((2 * stored, width), decoder.dtype),
                pltpu.VMEM((8, feats), jnp.float32),
                pltpu.VMEM((n, 8, feats), jnp.float32),
                pltpu.VMEM((n, 2 * cap, width // n), decoder.dtype),
                pltpu.VMEM((n, 2 * cap, width // n), decoder.dtype),
                pltpu.VMEM((n, cap, feats), jnp.float32),
                pltpu.VMEM((n, cap, feats), jnp.float32),
                pltpu.VMEM((8, feats), jnp.float32),
                pltpu.VMEM((n, 8, feats), jnp.float32),
                pltpu.SemaphoreType.DMA((2,)),
                pltpu.SemaphoreType.DMA((4, n)),
                pltpu.SemaphoreType.DMA((4, n)),
            ],
            compiler_params=pltpu.CompilerParams(
                collective_id=0, has_side_effects=True, vmem_limit_bytes=40 * 1024 * 1024
            ),
        )(ids, layers, acts, owner_map, kept, decoder, encoder)

    split = P(("groups", "row"))
    wide = P(("groups", "row"), None)
    return jax.shard_map(
        shards,
        mesh=mesh,
        in_specs=(split, split, split, P("groups", None), P("groups"), wide, wide),
        out_specs=(wide, wide),
        check_vma=False,
    )
```

```python
import functools

import jax
import jax.numpy as jnp
from jax import lax
from jax.experimental import pallas as pl
from jax.experimental.pallas import tpu as pltpu
from jax.sharding import PartitionSpec as P

MESH = pl.DeviceIdType.MESH


def partner(me, m, n):
    if n & (n - 1):
        return lax.rem(me + m, n)
    other, digit = me, 1
    while digit < n:
        if m & digit:
            other = other + digit - 2 * digit * lax.rem(me // digit, 2)
        digit *= 2
    return other


def far_first(n):
    return list(range(n // 2, n)) + list(range(n // 2 - 1, 0, -1))


def iota(shape, axis):
    return lax.broadcasted_iota(jnp.int32, shape, axis)


def kernel(
    n,
    ids_hbm,
    layers_hbm,
    acts_hbm,
    map_hbm,
    kept_ref,
    dec_ref,
    enc_ref,
    edges_ref,
    weights_ref,
    ids_ref,
    layers_ref,
    acts_ref,
    map_ref,
    stored_vm,
    meta_out,
    meta_in,
    rows_out,
    rows_in,
    part_out,
    part_in,
    total_out,
    total_in,
    load_sem,
    send_sem,
    recv_sem,
):
    me = lax.axis_index("row")
    mine = ids_ref.shape[0]
    stored, width = dec_ref.shape
    feats = n * mine
    cap = 2 * mine
    chunk = width // n
    offsets = far_first(n)

    loads = [
        pltpu.make_async_copy(dec_ref, stored_vm.at[pl.ds(0, stored)], load_sem.at[0]),
        pltpu.make_async_copy(enc_ref, stored_vm.at[pl.ds(stored, stored)], load_sem.at[1]),
    ]
    small = [
        pltpu.make_async_copy(source, target, load_sem.at[2 + i])
        for i, (source, target) in enumerate(
            [(ids_hbm, ids_ref), (map_hbm, map_ref), (layers_hbm, layers_ref), (acts_hbm, acts_ref)]
        )
    ]
    for load in small + loads:
        load.start()

    barrier = pltpu.get_barrier_semaphore()
    for m in offsets:
        pl.semaphore_signal(
            barrier, inc=1, device_id={"row": partner(me, m, n)}, device_id_type=MESH
        )

    lane = iota((8, feats), 1)
    field = iota((8, feats), 0)
    block = jnp.zeros((8, feats), jnp.float32)
    for load in small:
        load.wait()
    for k in range(mine):
        slot = map_ref[ids_ref[k]]
        here = lane == me * mine + k
        whole = jnp.where(
            field == 0, slot // stored, jnp.where(field == 1, slot % stored, layers_ref[k])
        ).astype(jnp.float32)
        block = jnp.where(here, jnp.where(field == 3, acts_ref[k], whole), block)
    meta_out[...] = block
    meta_in[me] = block

    pl.semaphore_wait(barrier, n - 1)

    def exchange(phase, source, target):
        copies = []
        for m in offsets:
            copy = pltpu.make_async_remote_copy(
                src_ref=source(partner(me, m, n)),
                dst_ref=target,
                send_sem=send_sem.at[phase, m],
                recv_sem=recv_sem.at[phase, m],
                device_id={"row": partner(me, m, n)},
                device_id_type=MESH,
            )
            copy.start()
            copies.append(copy)
        return copies

    first = exchange(0, lambda p: meta_out, meta_in.at[me])
    before = (iota((feats, feats), 0) < iota((feats, feats), 1)).astype(jnp.bfloat16)
    for copy in first:
        copy.wait_recv()
    meta = jnp.sum(meta_in[...], axis=0)
    owner = meta[0:1].astype(jnp.int32)
    local = meta[1:2].astype(jnp.int32)
    layer = meta[2:3]
    act = meta[3:4]
    by_owner = (jnp.broadcast_to(owner, (n, feats)) == iota((n, feats), 0)).astype(jnp.float32)
    earlier = jnp.dot(by_owner.astype(jnp.bfloat16), before, preferred_element_type=jnp.float32)
    place = jnp.sum(by_owner * earlier, axis=0, keepdims=True).astype(jnp.int32)
    packed = jnp.where(owner == me, place, -1)
    chosen = jnp.broadcast_to(packed, (cap, feats)) == iota((cap, feats), 0)
    pick = jnp.sum(
        jnp.where(chosen, jnp.broadcast_to(local + 1, (cap, feats)).astype(jnp.float32), 0.0),
        axis=1,
        keepdims=True,
    )
    pick = jnp.concatenate([pick, pick], axis=0)
    column = iota((2 * cap, 2 * stored), 1)
    second = iota((2 * cap, 2 * stored), 0) >= cap
    sought = jnp.where(second, column - stored, column) + 1
    sought = jnp.where(sought <= 0, -1, jnp.where(sought > stored, -1, sought))
    select = (
        jnp.broadcast_to(pick, (2 * cap, 2 * stored)) == sought.astype(jnp.float32)
    ).astype(jnp.bfloat16)

    for load in loads:
        load.wait()

    def selected(p):
        return jnp.dot(
            select,
            stored_vm[:, pl.ds(pl.multiple_of(p * chunk, chunk), chunk)],
            preferred_element_type=jnp.float32,
        ).astype(jnp.bfloat16)

    def take_and_give(p):
        rows_out[p] = selected(p)
        return rows_out.at[p]

    bulk = exchange(1, take_and_give, rows_in.at[me])
    rows_in[me] = selected(me)

    column_tiles, tiles = kept_ref.shape
    kept = jnp.transpose(kept_ref[...])
    spread = jnp.zeros((tiles, feats), jnp.int32)
    for c in range(column_tiles):
        within = iota((tiles, feats), 1) // (feats // column_tiles) == c
        spread = jnp.where(within, jnp.broadcast_to(kept[:, c : c + 1], (tiles, feats)), spread)
    spread = jnp.broadcast_to(spread[:, None, :], (tiles, mine, feats)).reshape(feats, feats)
    layer_down = jnp.transpose(jnp.broadcast_to(layer, (feats, feats)))
    allowed = jnp.where(
        layer_down < jnp.broadcast_to(layer, (feats, feats)),
        jnp.where(spread > 0, 1.0, 0.0),
        0.0,
    )
    count = jnp.sum(allowed, axis=0, keepdims=True)
    chosen_f = jnp.where(chosen, 1.0, 0.0)
    allowed_mine = jnp.dot(
        chosen_f.astype(jnp.bfloat16),
        allowed.astype(jnp.bfloat16),
        preferred_element_type=jnp.float32,
    )
    act_mine = jnp.sum(chosen_f * act, axis=1, keepdims=True)
    place_of = owner * cap + place
    position = (
        jnp.broadcast_to(place_of, (n * cap, feats)) == iota((n * cap, feats), 0)
    ).astype(jnp.float32)
    ordering = jnp.transpose(position).astype(jnp.bfloat16)

    for copy in bulk:
        copy.wait_recv()
    sources = rows_in[:, :cap, :].reshape(n * cap, chunk)
    targets = rows_in[:, cap:, :].reshape(n * cap, chunk)
    targets = jnp.dot(ordering, targets, preferred_element_type=jnp.float32).astype(jnp.bfloat16)
    part = lax.dot_general(
        sources, targets, (((1,), (1,)), ((), ())), preferred_element_type=jnp.float32
    )
    part_out[...] = part.reshape(n, cap, feats)
    sums = exchange(2, lambda p: part_out.at[p], part_in.at[me])
    part_in[me] = part_out[me]
    for copy in sums:
        copy.wait_recv()
    dots = jnp.sum(part_in[...], axis=0)
    edges = jnp.where(allowed_mine > 0.0, act_mine * dots, 0.0)
    edges_ref[...] = edges
    magnitude = jnp.abs(edges)
    partial = jnp.sum(magnitude.reshape(cap // 8, 8, feats), axis=0)
    total_out[...] = partial
    total_in[me] = partial
    totals = exchange(3, lambda p: total_out, total_in.at[me])
    for copy in totals:
        copy.wait_recv()
    total = jnp.sum(jnp.sum(total_in[...], axis=0), axis=0, keepdims=True)
    weights_ref[...] = magnitude * jnp.maximum(count, 1.0) / jnp.maximum(total, 1.0)
    for copy in first + bulk + sums + totals:
        copy.wait_send()


def solution(mesh):
    n = mesh.shape["row"]

    def shards(ids, layers, acts, kept, owner_map, decoder, encoder):
        mine = ids.shape[0]
        stored, width = decoder.shape
        feats, cap = n * mine, 2 * mine
        vmem = pl.BlockSpec(memory_space=pltpu.VMEM)
        hbm = pl.BlockSpec(memory_space=pltpu.HBM)
        result = jax.ShapeDtypeStruct((cap, feats), jnp.float32)
        return pl.pallas_call(
            functools.partial(kernel, n),
            out_shape=(result, result),
            in_specs=[hbm, hbm, hbm, hbm, vmem, hbm, hbm],
            out_specs=(vmem, vmem),
            scratch_shapes=[
                pltpu.SMEM(ids.shape, jnp.int32),
                pltpu.SMEM(layers.shape, jnp.int32),
                pltpu.SMEM(acts.shape, jnp.float32),
                pltpu.SMEM(owner_map.shape, jnp.int32),
                pltpu.VMEM((2 * stored, width), decoder.dtype),
                pltpu.VMEM((8, feats), jnp.float32),
                pltpu.VMEM((n, 8, feats), jnp.float32),
                pltpu.VMEM((n, 2 * cap, width // n), decoder.dtype),
                pltpu.VMEM((n, 2 * cap, width // n), decoder.dtype),
                pltpu.VMEM((n, cap, feats), jnp.float32),
                pltpu.VMEM((n, cap, feats), jnp.float32),
                pltpu.VMEM((8, feats), jnp.float32),
                pltpu.VMEM((n, 8, feats), jnp.float32),
                pltpu.SemaphoreType.DMA((6,)),
                pltpu.SemaphoreType.DMA((4, n)),
                pltpu.SemaphoreType.DMA((4, n)),
            ],
            compiler_params=pltpu.CompilerParams(
                collective_id=0, has_side_effects=True, vmem_limit_bytes=64 * 1024 * 1024
            ),
        )(ids, layers, acts, owner_map, kept.T, decoder, encoder)

    split = P(("groups", "row"))
    wide = P(("groups", "row"), None)
    return jax.shard_map(
        shards,
        mesh=mesh,
        in_specs=(split, split, split, P("groups", None), P("groups"), wide, wide),
        out_specs=(wide, wide),
        check_vma=False,
    )
```

```python
import functools

import jax
import jax.numpy as jnp
from jax import lax
from jax.experimental import pallas as pl
from jax.experimental.pallas import tpu as pltpu
from jax.sharding import PartitionSpec as P

MESH = pl.DeviceIdType.MESH


def partner(me, m, n):
    other, digit = me, 1
    while digit < n:
        if m & digit:
            other = other + digit - 2 * digit * lax.rem(me // digit, 2)
        digit *= 2
    return other


def far_first(n):
    return list(range(n // 2, n)) + list(range(n // 2 - 1, 0, -1))


def iota(shape, axis):
    return lax.broadcasted_iota(jnp.int32, shape, axis)


def kernel(
    n,
    ids_hbm,
    layers_hbm,
    acts_hbm,
    map_hbm,
    kept_ref,
    dec_ref,
    enc_ref,
    both_ref,
    ids_ref,
    layers_ref,
    acts_ref,
    map_ref,
    stored_vm,
    meta_out,
    meta_in,
    rows_out,
    near_in,
    far_in,
    part_out,
    part_in,
    total_out,
    total_in,
    load_sem,
    send_sem,
    recv_sem,
):
    me = lax.axis_index("row")
    mine = ids_ref.shape[0]
    stored, width = dec_ref.shape
    feats = n * mine
    cap = 2 * mine
    half = n // 2
    spot = lax.rem(me, half)
    chunk = width // half
    offsets = far_first(n)
    across = [m for m in offsets if m >= half]
    within = [m for m in offsets if m < half]

    loads = [
        pltpu.make_async_copy(dec_ref, stored_vm.at[pl.ds(0, stored)], load_sem.at[0]),
        pltpu.make_async_copy(enc_ref, stored_vm.at[pl.ds(stored, stored)], load_sem.at[1]),
    ]
    small = [
        pltpu.make_async_copy(source, target, load_sem.at[2 + i])
        for i, (source, target) in enumerate(
            [(ids_hbm, ids_ref), (map_hbm, map_ref), (layers_hbm, layers_ref), (acts_hbm, acts_ref)]
        )
    ]
    for load in small + loads:
        load.start()

    barrier = pltpu.get_barrier_semaphore()
    for m in offsets:
        pl.semaphore_signal(
            barrier, inc=1, device_id={"row": partner(me, m, n)}, device_id_type=MESH
        )

    lane = iota((8, feats), 1)
    field = iota((8, feats), 0)
    block = jnp.zeros((8, feats), jnp.float32)
    for load in small:
        load.wait()
    for k in range(mine):
        slot = map_ref[ids_ref[k]]
        here = lane == me * mine + k
        whole = jnp.where(
            field == 0, slot // stored, jnp.where(field == 1, slot % stored, layers_ref[k])
        ).astype(jnp.float32)
        block = jnp.where(here, jnp.where(field == 3, acts_ref[k], whole), block)
    meta_out[...] = block
    meta_in[me] = block

    pl.semaphore_wait(barrier, n - 1)

    def exchange(phase, partners, source, target):
        copies = []
        for m in partners:
            copy = pltpu.make_async_remote_copy(
                src_ref=source(partner(me, m, n)),
                dst_ref=target,
                send_sem=send_sem.at[phase, m],
                recv_sem=recv_sem.at[phase, m],
                device_id={"row": partner(me, m, n)},
                device_id_type=MESH,
            )
            copy.start()
            copies.append(copy)
        return copies

    first = exchange(0, offsets, lambda peer: meta_out, meta_in.at[me])
    before = (iota((feats, feats), 0) < iota((feats, feats), 1)).astype(jnp.bfloat16)
    for copy in first:
        copy.wait_recv()
    meta = jnp.sum(meta_in[...], axis=0)
    owner = meta[0:1].astype(jnp.int32)
    local = meta[1:2].astype(jnp.int32)
    layer = meta[2:3]
    act = meta[3:4]
    by_owner = (jnp.broadcast_to(owner, (n, feats)) == iota((n, feats), 0)).astype(jnp.float32)
    earlier = jnp.dot(by_owner.astype(jnp.bfloat16), before, preferred_element_type=jnp.float32)
    place = jnp.sum(by_owner * earlier, axis=0, keepdims=True).astype(jnp.int32)
    packed = jnp.where(owner == me, place, -1)
    chosen = jnp.broadcast_to(packed, (cap, feats)) == iota((cap, feats), 0)
    pick = jnp.sum(
        jnp.where(chosen, jnp.broadcast_to(local + 1, (cap, feats)).astype(jnp.float32), 0.0),
        axis=1,
        keepdims=True,
    )
    pick = jnp.concatenate([pick, pick], axis=0)
    column = iota((2 * cap, 2 * stored), 1)
    second = iota((2 * cap, 2 * stored), 0) >= cap
    sought = jnp.where(second, column - stored, column) + 1
    sought = jnp.where(sought <= 0, -1, jnp.where(sought > stored, -1, sought))
    select = (
        jnp.broadcast_to(pick, (2 * cap, 2 * stored)) == sought.astype(jnp.float32)
    ).astype(jnp.bfloat16)

    for load in loads:
        load.wait()

    def selected(p):
        return jnp.dot(
            select,
            stored_vm[:, pl.ds(pl.multiple_of(p * chunk, chunk), chunk)],
            preferred_element_type=jnp.float32,
        ).astype(jnp.bfloat16)

    def far_rows(peer):
        p = lax.rem(peer, half)
        rows_out[p] = selected(p)
        return rows_out.at[p, pl.ds(cap, cap)]

    bulk = exchange(1, across, far_rows, far_in.at[spot])
    bulk += exchange(1, within, lambda peer: rows_out.at[lax.rem(peer, half)], near_in.at[spot])
    near_in[spot] = rows_out[spot]

    column_tiles, tiles = kept_ref.shape
    kept = jnp.transpose(kept_ref[...])
    spread = jnp.zeros((tiles, feats), jnp.int32)
    for c in range(column_tiles):
        inside = iota((tiles, feats), 1) // (feats // column_tiles) == c
        spread = jnp.where(inside, jnp.broadcast_to(kept[:, c : c + 1], (tiles, feats)), spread)
    spread = jnp.broadcast_to(spread[:, None, :], (tiles, mine, feats)).reshape(feats, feats)
    layer_down = jnp.transpose(jnp.broadcast_to(layer, (feats, feats)))
    allowed = jnp.where(
        layer_down < jnp.broadcast_to(layer, (feats, feats)),
        jnp.where(spread > 0, 1.0, 0.0),
        0.0,
    )
    count = jnp.sum(allowed, axis=0, keepdims=True)
    chosen_f = jnp.where(chosen, 1.0, 0.0)
    allowed_mine = jnp.dot(
        chosen_f.astype(jnp.bfloat16),
        allowed.astype(jnp.bfloat16),
        preferred_element_type=jnp.float32,
    )
    act_mine = jnp.sum(chosen_f * act, axis=1, keepdims=True)
    away = jnp.where(owner // half == me // half, 0, half)
    place_of = (away + owner % half) * cap + place
    position = (
        jnp.broadcast_to(place_of, (n * cap, feats)) == iota((n * cap, feats), 0)
    ).astype(jnp.float32)
    ordering = jnp.transpose(position).astype(jnp.bfloat16)

    for copy in bulk:
        copy.wait_recv()
    sources = near_in[:, :cap, :].reshape(half * cap, chunk)
    targets = jnp.dot(
        ordering[:, : half * cap],
        near_in[:, cap:, :].reshape(half * cap, chunk),
        preferred_element_type=jnp.float32,
    )
    targets += jnp.dot(
        ordering[:, half * cap :],
        far_in[...].reshape(half * cap, chunk),
        preferred_element_type=jnp.float32,
    )
    targets = targets.astype(jnp.bfloat16)
    part = lax.dot_general(
        sources, targets, (((1,), (1,)), ((), ())), preferred_element_type=jnp.float32
    )
    part_out[...] = part.reshape(half, cap, feats)
    sums = exchange(2, within, lambda peer: part_out.at[lax.rem(peer, half)], part_in.at[spot])
    part_in[spot] = part_out[spot]
    for copy in sums:
        copy.wait_recv()
    dots = jnp.sum(part_in[...], axis=0)
    edges = jnp.where(allowed_mine > 0.0, act_mine * dots, 0.0)
    both_ref[0] = edges
    magnitude = jnp.abs(edges)
    partial = jnp.sum(magnitude.reshape(cap // 8, 8, feats), axis=0)
    total_out[...] = partial
    total_in[me] = partial
    totals = exchange(3, offsets, lambda peer: total_out, total_in.at[me])
    for copy in totals:
        copy.wait_recv()
    total = jnp.sum(jnp.sum(total_in[...], axis=0), axis=0, keepdims=True)
    both_ref[1] = magnitude * jnp.maximum(count, 1.0) / jnp.maximum(total, 1.0)
    for copy in first + bulk + sums + totals:
        copy.wait_send()


def solution(mesh):
    n = mesh.shape["row"]

    def shards(ids, layers, acts, kept, owner_map, decoder, encoder):
        mine = ids.shape[0]
        stored, width = decoder.shape
        feats, cap, half = n * mine, 2 * mine, n // 2
        chunk = width // half
        vmem = pl.BlockSpec(memory_space=pltpu.VMEM)
        hbm = pl.BlockSpec(memory_space=pltpu.HBM)
        result = jax.ShapeDtypeStruct((cap, feats), jnp.float32)
        both = pl.pallas_call(
            functools.partial(kernel, n),
            out_shape=jax.ShapeDtypeStruct((2, cap, feats), jnp.float32),
            in_specs=[hbm, hbm, hbm, hbm, vmem, hbm, hbm],
            out_specs=vmem,
            scratch_shapes=[
                pltpu.SMEM(ids.shape, jnp.int32),
                pltpu.SMEM(layers.shape, jnp.int32),
                pltpu.SMEM(acts.shape, jnp.float32),
                pltpu.SMEM(owner_map.shape, jnp.int32),
                pltpu.VMEM((2 * stored, width), decoder.dtype),
                pltpu.VMEM((8, feats), jnp.float32),
                pltpu.VMEM((n, 8, feats), jnp.float32),
                pltpu.VMEM((half, 2 * cap, chunk), decoder.dtype),
                pltpu.VMEM((half, 2 * cap, chunk), decoder.dtype),
                pltpu.VMEM((half, cap, chunk), decoder.dtype),
                pltpu.VMEM((half, cap, feats), jnp.float32),
                pltpu.VMEM((half, cap, feats), jnp.float32),
                pltpu.VMEM((8, feats), jnp.float32),
                pltpu.VMEM((n, 8, feats), jnp.float32),
                pltpu.SemaphoreType.DMA((6,)),
                pltpu.SemaphoreType.DMA((4, n)),
                pltpu.SemaphoreType.DMA((4, n)),
            ],
            compiler_params=pltpu.CompilerParams(
                collective_id=0, has_side_effects=True, vmem_limit_bytes=64 * 1024 * 1024
            ),
        )(ids, layers, acts, owner_map, kept.T, decoder, encoder)
        return both[0], both[1]

    split = P(("groups", "row"))
    wide = P(("groups", "row"), None)
    return jax.shard_map(
        shards,
        mesh=mesh,
        in_specs=(split, split, split, P("groups", None), P("groups"), wide, wide),
        out_specs=(wide, wide),
        check_vma=False,
    )
```

```python
import functools

import jax
import jax.numpy as jnp
from jax import lax
from jax.experimental import pallas as pl
from jax.experimental.pallas import tpu as pltpu
from jax.sharding import PartitionSpec as P

MESH = pl.DeviceIdType.MESH


def partner(me, m, n):
    other, digit = me, 1
    while digit < n:
        if m & digit:
            other = other + digit - 2 * digit * lax.rem(me // digit, 2)
        digit *= 2
    return other


def far_first(n):
    return list(range(n // 2, n)) + list(range(n // 2 - 1, 0, -1))


def iota(shape, axis):
    return lax.broadcasted_iota(jnp.int32, shape, axis)


def kernel(
    n,
    ids_hbm,
    layers_hbm,
    acts_hbm,
    map_hbm,
    kept_ref,
    dec_ref,
    enc_ref,
    both_ref,
    ids_ref,
    layers_ref,
    acts_ref,
    map_ref,
    stored_vm,
    meta_out,
    meta_in,
    rows_out,
    near_in,
    far_in,
    part_out,
    part_in,
    total_out,
    total_in,
    load_sem,
    send_sem,
    recv_sem,
):
    me = lax.axis_index("row")
    mine = ids_ref.shape[0]
    stored, width = dec_ref.shape
    feats = n * mine
    cap = 2 * mine
    half = n // 2
    spot = lax.rem(me, half)
    chunk = width // half
    offsets = far_first(n)
    across = [m for m in offsets if m >= half]
    within = [m for m in offsets if m < half]

    loads = [
        pltpu.make_async_copy(dec_ref, stored_vm.at[pl.ds(0, stored)], load_sem.at[0]),
        pltpu.make_async_copy(enc_ref, stored_vm.at[pl.ds(stored, stored)], load_sem.at[1]),
    ]
    small = [
        pltpu.make_async_copy(source, target, load_sem.at[2 + i])
        for i, (source, target) in enumerate(
            [(ids_hbm, ids_ref), (map_hbm, map_ref), (layers_hbm, layers_ref), (acts_hbm, acts_ref)]
        )
    ]
    for load in small + loads:
        load.start()

    barrier = pltpu.get_barrier_semaphore()
    for m in offsets:
        pl.semaphore_signal(
            barrier, inc=1, device_id={"row": partner(me, m, n)}, device_id_type=MESH
        )

    lane = iota((4, feats), 1)
    field = iota((4, feats), 0)
    block = jnp.zeros((4, feats), jnp.float32)
    for load in small:
        load.wait()
    for k in range(mine):
        slot = map_ref[ids_ref[k]]
        here = lane == me * mine + k
        whole = jnp.where(
            field == 0, slot // stored, jnp.where(field == 1, slot % stored, layers_ref[k])
        ).astype(jnp.float32)
        block = jnp.where(here, jnp.where(field == 3, acts_ref[k], whole), block)
    meta_out[...] = block
    meta_in[me] = block

    pl.semaphore_wait(barrier, n - 1)

    def exchange(phase, partners, source, target):
        copies = []
        for m in partners:
            copy = pltpu.make_async_remote_copy(
                src_ref=source(partner(me, m, n)),
                dst_ref=target,
                send_sem=send_sem.at[phase, m],
                recv_sem=recv_sem.at[phase, m],
                device_id={"row": partner(me, m, n)},
                device_id_type=MESH,
            )
            copy.start()
            copies.append(copy)
        return copies

    first = exchange(0, offsets, lambda peer: meta_out, meta_in.at[me])
    before = (iota((feats, feats), 0) < iota((feats, feats), 1)).astype(jnp.bfloat16)
    for copy in first:
        copy.wait_recv()
    meta = jnp.sum(meta_in[...], axis=0)
    owner = meta[0:1].astype(jnp.int32)
    local = meta[1:2].astype(jnp.int32)
    layer = meta[2:3]
    act = meta[3:4]
    by_owner = (jnp.broadcast_to(owner, (n, feats)) == iota((n, feats), 0)).astype(jnp.float32)
    earlier = jnp.dot(by_owner.astype(jnp.bfloat16), before, preferred_element_type=jnp.float32)
    place = jnp.sum(by_owner * earlier, axis=0, keepdims=True).astype(jnp.int32)
    packed = jnp.where(owner == me, place, -1)
    chosen = jnp.broadcast_to(packed, (cap, feats)) == iota((cap, feats), 0)
    pick = jnp.sum(
        jnp.where(chosen, jnp.broadcast_to(local + 1, (cap, feats)).astype(jnp.float32), 0.0),
        axis=1,
        keepdims=True,
    )
    pick = jnp.concatenate([pick, pick], axis=0)
    column = iota((2 * cap, 2 * stored), 1)
    second = iota((2 * cap, 2 * stored), 0) >= cap
    sought = jnp.where(second, column - stored, column) + 1
    sought = jnp.where(sought <= 0, -1, jnp.where(sought > stored, -1, sought))
    select = (
        jnp.broadcast_to(pick, (2 * cap, 2 * stored)) == sought.astype(jnp.float32)
    ).astype(jnp.bfloat16)

    for load in loads:
        load.wait()

    def selected(p):
        return jnp.dot(
            select,
            stored_vm[:, pl.ds(pl.multiple_of(p * chunk, chunk), chunk)],
            preferred_element_type=jnp.float32,
        ).astype(jnp.bfloat16)

    def far_rows(peer):
        p = lax.rem(peer, half)
        rows_out[p] = selected(p)
        return rows_out.at[p, pl.ds(cap, cap)]

    bulk = exchange(1, across, far_rows, far_in.at[spot])
    bulk += exchange(1, within, lambda peer: rows_out.at[lax.rem(peer, half)], near_in.at[spot])
    near_in[spot] = rows_out[spot]

    column_tiles, tiles = kept_ref.shape
    kept = jnp.transpose(kept_ref[...])
    spread = jnp.zeros((tiles, feats), jnp.int32)
    for c in range(column_tiles):
        inside = iota((tiles, feats), 1) // (feats // column_tiles) == c
        spread = jnp.where(inside, jnp.broadcast_to(kept[:, c : c + 1], (tiles, feats)), spread)
    spread = jnp.broadcast_to(spread[:, None, :], (tiles, mine, feats)).reshape(feats, feats)
    layer_down = jnp.transpose(jnp.broadcast_to(layer, (feats, feats)))
    allowed = jnp.where(
        layer_down < jnp.broadcast_to(layer, (feats, feats)),
        jnp.where(spread > 0, 1.0, 0.0),
        0.0,
    )
    count = jnp.sum(allowed, axis=0, keepdims=True)
    chosen_f = jnp.where(chosen, 1.0, 0.0)
    allowed_mine = jnp.dot(
        chosen_f.astype(jnp.bfloat16),
        allowed.astype(jnp.bfloat16),
        preferred_element_type=jnp.float32,
    )
    act_mine = jnp.sum(chosen_f * act, axis=1, keepdims=True)
    away = jnp.where(owner // half == me // half, 0, half)
    place_of = (away + owner % half) * cap + place
    position = (
        jnp.broadcast_to(place_of, (n * cap, feats)) == iota((n * cap, feats), 0)
    ).astype(jnp.float32)
    ordering = jnp.transpose(position).astype(jnp.bfloat16)

    for copy in bulk:
        copy.wait_recv()
    sources = near_in[:, :cap, :].reshape(half * cap, chunk)
    targets = jnp.dot(
        ordering[:, : half * cap],
        near_in[:, cap:, :].reshape(half * cap, chunk),
        preferred_element_type=jnp.float32,
    )
    targets += jnp.dot(
        ordering[:, half * cap :],
        far_in[...].reshape(half * cap, chunk),
        preferred_element_type=jnp.float32,
    )
    targets = targets.astype(jnp.bfloat16)
    part = lax.dot_general(
        sources, targets, (((1,), (1,)), ((), ())), preferred_element_type=jnp.float32
    )
    part_out[...] = part.reshape(half, cap, feats)
    sums = exchange(2, within, lambda peer: part_out.at[lax.rem(peer, half)], part_in.at[spot])
    part_in[spot] = part_out[spot]
    for copy in sums:
        copy.wait_recv()
    dots = jnp.sum(part_in[...], axis=0)
    edges = jnp.where(allowed_mine > 0.0, act_mine * dots, 0.0)
    both_ref[0] = edges
    magnitude = jnp.abs(edges)
    partial = jnp.sum(magnitude, axis=0, keepdims=True)
    total_out[...] = partial
    total_in[me] = partial
    totals = exchange(3, offsets, lambda peer: total_out, total_in.at[me])
    for copy in totals:
        copy.wait_recv()
    total = jnp.sum(total_in[...], axis=0)
    both_ref[1] = magnitude * jnp.maximum(count, 1.0) / jnp.maximum(total, 1.0)
    for copy in first + bulk + sums + totals:
        copy.wait_send()


def solution(mesh):
    n = mesh.shape["row"]

    def shards(ids, layers, acts, kept, owner_map, decoder, encoder):
        mine = ids.shape[0]
        stored, width = decoder.shape
        feats, cap, half = n * mine, 2 * mine, n // 2
        chunk = width // half
        vmem = pl.BlockSpec(memory_space=pltpu.VMEM)
        hbm = pl.BlockSpec(memory_space=pltpu.HBM)
        both = pl.pallas_call(
            functools.partial(kernel, n),
            out_shape=pltpu.VMEM((2, cap, feats), jnp.float32),
            in_specs=[hbm, hbm, hbm, hbm, vmem, hbm, hbm],
            out_specs=vmem,
            scratch_shapes=[
                pltpu.SMEM(ids.shape, jnp.int32),
                pltpu.SMEM(layers.shape, jnp.int32),
                pltpu.SMEM(acts.shape, jnp.float32),
                pltpu.SMEM(owner_map.shape, jnp.int32),
                pltpu.VMEM((2 * stored, width), decoder.dtype),
                pltpu.VMEM((4, feats), jnp.float32),
                pltpu.VMEM((n, 4, feats), jnp.float32),
                pltpu.VMEM((half, 2 * cap, chunk), decoder.dtype),
                pltpu.VMEM((half, 2 * cap, chunk), decoder.dtype),
                pltpu.VMEM((half, cap, chunk), decoder.dtype),
                pltpu.VMEM((half, cap, feats), jnp.float32),
                pltpu.VMEM((half, cap, feats), jnp.float32),
                pltpu.VMEM((1, feats), jnp.float32),
                pltpu.VMEM((n, 1, feats), jnp.float32),
                pltpu.SemaphoreType.DMA((6,)),
                pltpu.SemaphoreType.DMA((4, n)),
                pltpu.SemaphoreType.DMA((4, n)),
            ],
            compiler_params=pltpu.CompilerParams(
                collective_id=0, has_side_effects=True, vmem_limit_bytes=56 * 1024 * 1024
            ),
        )(ids, layers, acts, owner_map, kept.T, decoder, encoder)
        return both[0], both[1]

    split = P(("groups", "row"))
    wide = P(("groups", "row"), None)
    return jax.shard_map(
        shards,
        mesh=mesh,
        in_specs=(split, split, split, P("groups", None), P("groups"), wide, wide),
        out_specs=(wide, wide),
        check_vma=False,
    )
```
